256 devices in a mesh: dp: 16 (over z_lo, x, core), cp: 16 (over y, z_hi).
Axes of the slice: x: 4, y: 4, z: 8 (z_hi: 4, z_lo: 2; z = z_hi * 2 + z_lo), core: 2. Of those that a mesh axis runs over, the one named last changes fastest.
Arguments:
- queries: bfloat16 [65536, 4096], P(('dp', 'cp')), may hold values from -128 to 128
- keys: bfloat16 [65536, 1024], P(('dp', 'cp')), may hold values from -6 to 6
- values: bfloat16 [65536, 1024], P(('dp', 'cp')), may hold values from -6 to 6
- grad_out: bfloat16 [65536, 4096], P(('dp', 'cp')), may hold values from -6 to 6
- segment_ids: int32 [65536], replicated, may hold values from 0 to 169, never falling along the last dimension, each value on 1 to 768 neighbouring positions
Outputs:
- attended: bfloat16 [65536, 4096], P(('dp', 'cp'))
- grad_queries: bfloat16 [65536, 4096], P(('dp', 'cp'))
- grad_keys: bfloat16 [65536, 1024], P(('dp', 'cp'))
- grad_values: bfloat16 [65536, 1024], P(('dp', 'cp'))
The draws below stay inside these ranges and needn't reach their ends.
Inputs may be any that keep to these rules, and one draw needn't show every extreme that they name: `segment_ids`: document ids never fall along the packed tokens; each document holds 1 to 768 tokens and one holds exactly 768.
All inputs are finite; a program needn't handle non-finite values.
Results may differ from the reference program's by a relative error of at most 0.018.
Values may be sent and summed in bfloat16 or wider, within the bound.
No kernel may reach another device: no remote copies, remote signals or barrier semaphores. Data moves between devices by JAX's collectives and lax.ppermute only.
A program may use at most 128 MiB of HBM per device.

```python
import math
import jax
import jax.numpy as jnp
import numpy as np
from jax import lax

HQ = 32
HK = 8
HD = 128
TOK_DEV = 256
REACH = 3
TOKENS = 65536
MOST = 768
DOCS = 170


def key_base(key):
    return jnp.clip(jax.random.normal(key, (TOKENS, HK * HD), jnp.float32), -6.0, 6.0)


def draw_keys(key, part):
    shared = key_base(key)
    result = shared
    return result.astype(jnp.bfloat16)


def draw_queries(key, part):
    key = jax.random.fold_in(key, 7)
    result = jnp.clip(jax.random.normal(key, (TOKENS, HQ * HD), jnp.float32), -6.0, 6.0)
    return result.astype(jnp.bfloat16)


def level_of(stream_key, shape, shards, low, high):
    factor_of, own = 1.0, jax.random.fold_in(stream_key, 6)
    for dim, parts in shards:
        steps = jnp.exp(jax.random.uniform(jax.random.fold_in(own, dim), (parts,), jnp.float32, low / len(shards), high / len(shards)))
        factor_of = factor_of * jnp.repeat(steps, shape[dim] // parts).reshape([-1 if axis == dim else 1 for axis in range(len(shape))])
    return factor_of


def split_up(number_of, total, reach, lean):
    portions = [(1 << 20) // math.isqrt(standing ** lean) + 1 for standing in range(2, number_of + 1)]
    rest, given = total - reach - (number_of - 1), [1] * (number_of - 1)
    while rest > 0:
        movable = [i for i in range(number_of - 1) if given[i] < reach]
        mass, left = sum([portions[i] for i in movable]), rest
        for i in movable:
            extra = min(reach - given[i], max(1, left * portions[i] // mass), rest)
            given[i] = given[i] + extra
            rest = rest - extra
    return np.array([reach] + given)


def uneven(key, amount, total, most, slope):
    if amount == 2:
        one = jax.random.randint(key, (), max(1, total - most), min(most, total - 1) + 1)
        return jnp.stack([one, total - one])
    tallies = jnp.asarray(split_up(amount, total, most, slope), jnp.int32)
    couples = (amount - 1) // 2
    donor, taker = tallies[1:1 + 2 * couples:2], tallies[2:2 + 2 * couples:2]
    slack = jnp.minimum(donor - 1, most - taker)
    passed = jax.random.randint(jax.random.fold_in(key, 1), (couples,), 0, 1 << 20) % (slack + 1)
    tallies = tallies.at[1:1 + 2 * couples:2].set(donor - passed).at[2:2 + 2 * couples:2].set(taker + passed)
    return tallies[jax.random.permutation(jax.random.fold_in(key, 2), amount)]


def noise(rng, extent, spread, reach, cuts=(), held_as=jnp.bfloat16):
    level = level_of(rng, extent, cuts, -0.22, 0.18) if cuts else 1.0
    array = jax.random.normal(rng, extent, jnp.float32) * spread * level
    return jnp.minimum(jnp.maximum(array, -reach), reach).astype(held_as)


def setup_inputs(seed: int = 0) -> dict:
    arg_keys = jax.random.split(jax.random.key(seed), 6)
    queries = draw_queries(jax.random.fold_in(arg_keys[5], 71), 0)
    keys = draw_keys(jax.random.fold_in(arg_keys[5], 71), 0)
    values = noise(arg_keys[2], (TOKENS, HK * HD), 1.0, 6.0, ((0, 256),))
    grad_out = noise(arg_keys[3], (TOKENS, HQ * HD), 1.0, 6.0, ((0, 256),))
    segment_ids = jnp.searchsorted(jnp.cumsum(uneven(arg_keys[4], DOCS, TOKENS, MOST, 2)), jnp.arange(TOKENS), side="right").astype(jnp.int32)
    return dict(queries=queries, keys=keys, values=values, grad_out=grad_out, segment_ids=segment_ids)


def head_terms(inputs):
    query_part, key_part, value_part, grad_part, visible = inputs
    score_scale = HD ** -0.5
    scores = jnp.einsum('gtd,wd->gtw', query_part.astype(jnp.float32), key_part.astype(jnp.float32)) * score_scale
    scores = jnp.where(visible[None], scores, -jnp.inf)
    maximum = jnp.max(scores, axis=-1, keepdims=True)
    log_total = maximum + jnp.log(jnp.sum(jnp.exp(scores - maximum), axis=-1, keepdims=True))
    probability = jnp.exp(scores - log_total)
    prob_half = probability.astype(jnp.bfloat16)
    attended = jnp.einsum('gtw,wd->gtd', prob_half.astype(jnp.float32), value_part.astype(jnp.float32)).astype(jnp.bfloat16)
    row_delta = jnp.sum(grad_part.astype(jnp.float32) * attended.astype(jnp.float32), axis=-1, keepdims=True)
    grad_prob = jnp.einsum('gtd,wd->gtw', grad_part.astype(jnp.float32), value_part.astype(jnp.float32))
    grad_score = (probability * (grad_prob - row_delta)).astype(jnp.bfloat16)
    grad_query = (jnp.einsum('gtw,wd->gtd', grad_score.astype(jnp.float32), key_part.astype(jnp.float32)) * score_scale).astype(jnp.bfloat16)
    grad_key = jnp.einsum('gtw,gtd->wd', grad_score.astype(jnp.float32), query_part.astype(jnp.float32)) * score_scale
    grad_value = jnp.einsum('gtw,gtd->wd', prob_half.astype(jnp.float32), grad_part.astype(jnp.float32))
    return attended, grad_query, grad_key, grad_value


def attend_block(query_block, key_window, value_window, grad_block, seg_query, seg_window, first_row):
    query_rows = query_block.shape[0]
    window = key_window.shape[0]
    margin = window - query_rows
    groups = HQ // HK
    query_pos = first_row + jnp.arange(query_rows, dtype=jnp.int32)
    key_pos = first_row - margin + jnp.arange(window, dtype=jnp.int32)
    visible = (seg_query[:, None] == seg_window[None, :]) & (key_pos[None, :] <= query_pos[:, None])
    query_heads = query_block.reshape(query_rows, HK, groups, HD).transpose(1, 2, 0, 3)
    grad_heads = grad_block.reshape(query_rows, HK, groups, HD).transpose(1, 2, 0, 3)
    key_heads = key_window.reshape(window, HK, HD).transpose(1, 0, 2)
    value_heads = value_window.reshape(window, HK, HD).transpose(1, 0, 2)
    masks = jnp.broadcast_to(visible[None], (HK, query_rows, window))
    attended, grad_query, grad_key, grad_value = lax.map(head_terms, (query_heads, key_heads, value_heads, grad_heads, masks))
    attended = attended.transpose(2, 0, 1, 3).reshape(query_rows, HQ * HD)
    grad_query = grad_query.transpose(2, 0, 1, 3).reshape(query_rows, HQ * HD)
    grad_key = grad_key.transpose(1, 0, 2).reshape(window, HK * HD)
    grad_value = grad_value.transpose(1, 0, 2).reshape(window, HK * HD)
    return attended, grad_query, grad_key, grad_value


def reference(queries, keys, values, grad_out, segment_ids):
    margin = REACH * TOK_DEV
    window = margin + TOK_DEV
    key_pad = jnp.concatenate([jnp.zeros((margin, HK * HD), keys.dtype), keys], 0)
    value_pad = jnp.concatenate([jnp.zeros((margin, HK * HD), values.dtype), values], 0)
    seg_pad = jnp.concatenate([jnp.full((margin,), -1, jnp.int32), segment_ids.astype(jnp.int32)], 0)

    def advance(carry, block):
        grad_keys, grad_values = carry
        first_row = (block * TOK_DEV).astype(jnp.int32)
        query_block = lax.dynamic_slice_in_dim(queries, first_row, TOK_DEV, 0)
        grad_block = lax.dynamic_slice_in_dim(grad_out, first_row, TOK_DEV, 0)
        key_window = lax.dynamic_slice_in_dim(key_pad, first_row, window, 0)
        value_window = lax.dynamic_slice_in_dim(value_pad, first_row, window, 0)
        seg_query = lax.dynamic_slice_in_dim(segment_ids.astype(jnp.int32), first_row, TOK_DEV, 0)
        seg_window = lax.dynamic_slice_in_dim(seg_pad, first_row, window, 0)
        attended, grad_query, key_terms, value_terms = attend_block(query_block, key_window, value_window, grad_block, seg_query, seg_window, first_row)
        grad_keys = lax.dynamic_update_slice_in_dim(grad_keys, lax.dynamic_slice_in_dim(grad_keys, first_row, window, 0) + key_terms, first_row, 0)
        grad_values = lax.dynamic_update_slice_in_dim(grad_values, lax.dynamic_slice_in_dim(grad_values, first_row, window, 0) + value_terms, first_row, 0)
        return (grad_keys, grad_values), (attended, grad_query)

    zeros_pad = jnp.zeros((TOKENS + margin, HK * HD), jnp.float32)
    (grad_keys, grad_values), (attended, grad_queries) = lax.scan(advance, (zeros_pad, zeros_pad), jnp.arange(TOKENS // TOK_DEV, dtype=jnp.int32))
    attended = attended.reshape(TOKENS, HQ * HD)
    grad_queries = grad_queries.reshape(TOKENS, HQ * HD)
    return attended, grad_queries, grad_keys[margin:].astype(jnp.bfloat16), grad_values[margin:].astype(jnp.bfloat16)
```

```python
import functools

import jax
import jax.numpy as jnp
from jax import lax
from jax.experimental import pallas as pl
from jax.experimental.pallas import tpu as pltpu
from jax.sharding import PartitionSpec as P

HQ = 32
HK = 8
HD = 128
GROUP = HQ // HK
REACH = 3
BLOCKS = REACH + 1
AXES = ("dp", "cp")
LOG2E = 1.4426950408889634
HIDDEN = -1e30

CHUNKS = ((0, 2, 1), (2, 2, -1), (4, 2, 1), (6, 2, -1))


def moved(value, steps):
    count = lax.axis_size(AXES)
    return lax.ppermute(value, AXES, [(i, (i + steps) % count) for i in range(count)])


def dot_nt(a, b):
    return lax.dot_general(a, b, (((1,), (1,)), ((), ())), preferred_element_type=jnp.float32)


def dot_nn(a, b):
    return jnp.dot(a, b, preferred_element_type=jnp.float32)


def attend_kernel(heads, seg_col, seg_row, q, do, k0, v0, *refs):
    recv = refs[: 2 * REACH]
    att, dq, g0, g1, g2, g3, bias = refs[-7:]
    rows = q.shape[0]
    scale = HD**-0.5

    @pl.when(pl.program_id(0) == 0)
    def _():
        same = seg_col[...] == seg_row[...]
        query_pos = lax.broadcasted_iota(jnp.int32, same.shape, 0)
        key_pos = lax.broadcasted_iota(jnp.int32, same.shape, 1) - REACH * rows
        bias[...] = jnp.where(same & (key_pos <= query_pos), 0.0, HIDDEN)

    keys = [k0[...]] + [recv[2 * b][...] for b in range(REACH)]
    values = [v0[...]] + [recv[2 * b + 1][...] for b in range(REACH)]
    dk = [None] * BLOCKS
    dv = [None] * BLOCKS
    for g in range(GROUP):
        cols = slice(g * HD, (g + 1) * HD)
        qg = q[:, cols]
        dog = do[:, cols]
        t = []
        for b in range(BLOCKS):
            s = dot_nt(qg, keys[b]) * (scale * LOG2E)
            t.append(s + bias[:, (REACH - b) * rows : (BLOCKS - b) * rows])
        top = functools.reduce(jnp.maximum, t)
        top = jnp.max(top, axis=1, keepdims=True)
        e = [jnp.exp2(x - top) for x in t]
        total = jnp.sum(functools.reduce(jnp.add, e), axis=1, keepdims=True)
        inv = 1.0 / total
        p = [x * inv for x in e]
        ph = [x.astype(jnp.bfloat16) for x in p]
        out = functools.reduce(jnp.add, [dot_nn(ph[b], values[b]) for b in range(BLOCKS)])
        out = out.astype(jnp.bfloat16)
        att[:, cols] = out
        delta = jnp.sum(dog.astype(jnp.float32) * out.astype(jnp.float32), axis=1, keepdims=True)
        ds = [
            (p[b] * (dot_nt(dog, values[b]) - delta)).astype(jnp.bfloat16) for b in range(BLOCKS)
        ]
        dqg = functools.reduce(jnp.add, [dot_nn(ds[b], keys[b]) for b in range(BLOCKS)])
        dq[:, cols] = (dqg * scale).astype(jnp.bfloat16)
        qt = qg.T
        dot_ = dog.T
        for b in range(BLOCKS):
            a = dot_nn(qt, ds[b])
            c = dot_nn(dot_, ph[b])
            dk[b] = a if g == 0 else dk[b] + a
            dv[b] = c if g == 0 else dv[b] + c
    for b, ref in enumerate((g0, g1, g2, g3)):
        ref[0] = (dk[b] * scale).T.astype(ref.dtype)
        ref[1] = dv[b].T.astype(ref.dtype)


def attend(chunk, seg_col, seg_row, q, do, k, v, received, prev, far_first):
    first, heads, _ = chunk
    rows = q.shape[0]
    whole = lambda a: pl.BlockSpec(a.shape, lambda h: (0,) * a.ndim)
    wide = pl.BlockSpec((rows, GROUP * HD), lambda h: (0, first + h))
    own = pl.BlockSpec((rows, HD), lambda h: (0, first + h))
    got_k = pl.BlockSpec((None, rows, HD), lambda h: (0, 0, h))
    got_v = pl.BlockSpec((None, rows, HD), lambda h: (1, 0, h))
    in_specs = [whole(seg_col), whole(seg_row), wide, wide, own, own]
    args = [seg_col, seg_row, q, do, k, v]
    for block in received:
        in_specs += [got_k, got_v]
        args += [block, block]
    aliases = {}
    if prev is not None:
        aliases = {len(args): 0, len(args) + 1: 1}
        in_specs += [pl.BlockSpec(memory_space=pl.ANY)] * 2
        args += list(prev)
    terms = pl.BlockSpec((2, rows, HD), lambda h: (0, 0, h))
    term_types = [jnp.float32] * BLOCKS
    term_types[far_first] = jnp.bfloat16
    flops = 6 * 2 * rows * rows * BLOCKS * HD * GROUP * heads
    return pl.pallas_call(
        functools.partial(attend_kernel, heads),
        grid=(heads,),
        in_specs=in_specs,
        out_specs=[wide, wide] + [terms] * BLOCKS,
        out_shape=[jax.ShapeDtypeStruct(q.shape, q.dtype)] * 2
        + [jax.ShapeDtypeStruct((2, rows, heads * HD), t) for t in term_types],
        scratch_shapes=[pltpu.VMEM((rows, BLOCKS * rows), jnp.float32)],
        input_output_aliases=aliases,
        compiler_params=pltpu.CompilerParams(vmem_limit_bytes=48 * 1024 * 1024),
        cost_estimate=pl.CostEstimate(
            flops=flops, bytes_accessed=8 * 2**20, transcendentals=rows * rows * 4 * GROUP * heads
        ),
        name="attend",
    )(*args)


def shards(queries, keys, values, grad_out, segment_ids):
    rows = queries.shape[0]
    margin = REACH * rows
    first_row = lax.axis_index(AXES) * rows
    seg_pad = jnp.concatenate([jnp.full((margin,), -1, jnp.int32), segment_ids], 0)
    seg_row = lax.dynamic_slice_in_dim(seg_pad, first_row, margin + rows, 0)
    seg_col = seg_row[margin:].reshape(rows, 1)
    seg_row = seg_row.reshape(1, margin + rows)

    received = []
    for first, heads, way in CHUNKS:
        cols = slice(first * HD, (first + heads) * HD)
        pack = jnp.stack([keys[:, cols], values[:, cols]])
        if way > 0:
            one = moved(pack, 1)
            two = moved(one, 1)
            three = moved(two, 1)
        else:
            three = moved(pack, 3)
            two = moved(three, -1)
            one = moved(two, -1)
        received.append((one, two, three))

    prev = None
    grads = []
    for chunk, blocks in zip(CHUNKS, received):
        way = chunk[2]
        att, dq, g0, g1, g2, g3 = attend(
            chunk, seg_col, seg_row, queries, grad_out, keys, values, blocks, prev,
            3 if way > 0 else 1,
        )
        prev = (att, dq)
        if way > 0:
            t = moved(g3, -1)
            t = moved((g2 + t).astype(jnp.bfloat16), -1)
            t = moved((g1 + t).astype(jnp.bfloat16), -1)
        else:
            t = moved(g1, 1)
            t = moved((g2 + t).astype(jnp.bfloat16), 1)
            t = moved((g3 + t).astype(jnp.bfloat16), -3)
        grads.append((g0 + t).astype(jnp.bfloat16))
    grad_k = jnp.concatenate([g[0] for g in grads], 1)
    grad_v = jnp.concatenate([g[1] for g in grads], 1)
    return prev[0], prev[1], grad_k, grad_v


def solution(mesh):
    spec = P(AXES, None)
    return jax.shard_map(
        shards,
        mesh=mesh,
        in_specs=(spec, spec, spec, spec, P()),
        out_specs=(spec, spec, spec, spec),
        check_vma=False,
    )
```

```python
import functools

import jax
import jax.numpy as jnp
from jax import lax
from jax.experimental import pallas as pl
from jax.experimental.pallas import tpu as pltpu
from jax.sharding import PartitionSpec as P

HQ = 32
HK = 8
HD = 128
GROUP = HQ // HK
REACH = 3
BLOCKS = REACH + 1
AXES = ("dp", "cp")
LOG2E = 1.4426950408889634
HIDDEN = -1e30

GROUPS = ((0, 4), (4, 4))
CALLS = ((0, 0, 2), (0, 2, 2), (1, 0, 2), (1, 2, 2))


def moved(value, steps):
    count = lax.axis_size(AXES)
    return lax.ppermute(value, AXES, [(i, (i + steps) % count) for i in range(count)])


def after(value, gate):
    return lax.optimization_barrier((value, gate))[0]


def dot_nt(a, b):
    return lax.dot_general(a, b, (((1,), (1,)), ((), ())), preferred_element_type=jnp.float32)


def dot_nn(a, b):
    return jnp.dot(a, b, preferred_element_type=jnp.float32)


def attend_kernel(split, total, seg_col, seg_row, q, do, *refs):
    *outs, bias, kcat, vcat, scores, ph, ds = refs[2 * BLOCKS :]
    outs = outs[-(5 + (split > 0) + (split < total)) :]
    att, dq, own, keep, back1, *sent = outs
    rows = q.shape[0]
    scale = HD**-0.5

    @pl.when(pl.program_id(0) == 0)
    def _():
        for b in range(BLOCKS):
            at = (REACH - b) * rows
            seen = seg_col[...] == seg_row[:, at : at + rows]
            if b == 0:
                key_pos = lax.broadcasted_iota(jnp.int32, seen.shape, 1)
                seen &= key_pos <= lax.broadcasted_iota(jnp.int32, seen.shape, 0)
            bias[:, b * rows : (b + 1) * rows] = jnp.where(seen, 0.0, HIDDEN)

    for b in range(BLOCKS):
        kcat[b * rows : (b + 1) * rows, :] = refs[2 * b][...]
        vcat[b * rows : (b + 1) * rows, :] = refs[2 * b + 1][...]

    def score(g):
        qg = q[:, g * HD : (g + 1) * HD]
        scores[g % 2] = dot_nt(qg, kcat[...]) * (scale * LOG2E) + bias[...]

    def exponent(g):
        t = scores[g % 2]
        e = jnp.exp2(t - jnp.max(t, axis=1, keepdims=True))
        ph[g % 2] = e.astype(jnp.bfloat16)
        return 1.0 / jnp.sum(e, axis=1, keepdims=True)

    dk = dv = None
    score(0)
    inv = exponent(0)
    for g in range(GROUP):
        cols = slice(g * HD, (g + 1) * HD)
        if g + 1 < GROUP:
            score(g + 1)
        out = (dot_nn(ph[g % 2], vcat[...]) * inv).astype(jnp.bfloat16)
        att[:, cols] = out
        dog = (do[:, cols].astype(jnp.float32) * inv).astype(jnp.bfloat16)
        delta = jnp.sum(dog.astype(jnp.float32) * out.astype(jnp.float32), axis=1, keepdims=True)
        dp = dot_nt(dog, vcat[...])
        ds[g % 2] = (ph[g % 2].astype(jnp.float32) * (dp - delta)).astype(jnp.bfloat16)
        if g + 1 < GROUP:
            inv = exponent(g + 1)
        dq[:, cols] = (dot_nn(ds[g % 2], kcat[...]) * scale).astype(jnp.bfloat16)
        a, c = dot_nn(q[:, cols].T, ds[g % 2]), dot_nn(dog.T, ph[g % 2])
        dk = a if g == 0 else dk + a
        dv = c if g == 0 else dv + c

    def put(ref, b):
        at = slice(b * rows, (b + 1) * rows)
        ref[0, 0] = (dk[:, at] * scale).T.astype(ref.dtype)
        ref[0, 1] = dv[:, at].T.astype(ref.dtype)

    put(own, 0)

    def put_low():
        put(back1, 2)
        put(sent[0], 3)
        put(keep, 1)

    def put_high():
        put(back1, 1)
        put(sent[-1], 2)
        put(keep, 3)

    if split == total:
        put_low()
    elif split == 0:
        put_high()
    else:
        pl.when(pl.program_id(0) < split)(put_low)
        pl.when(pl.program_id(0) >= split)(put_high)


def attend(first, heads, split, seg_col, seg_row, q, do, k, v, received, prev):
    rows = q.shape[0]
    whole = lambda a: pl.BlockSpec(a.shape, lambda h: (0,) * a.ndim)
    wide = pl.BlockSpec((rows, GROUP * HD), lambda h: (0, first + h))
    own = pl.BlockSpec((rows, HD), lambda h: (0, first + h))
    in_specs = [whole(seg_col), whole(seg_row), wide, wide, own, own]
    args = [seg_col, seg_row, q, do, k, v]
    for block, at in received:
        for part in range(2):
            in_specs.append(
                pl.BlockSpec((None, rows, HD), lambda h, at=at, part=part: (part, 0, at + h))
            )
            args.append(block)
    aliases = {}
    if prev is not None:
        aliases = {len(args): 0, len(args) + 1: 1}
        in_specs += [pl.BlockSpec(memory_space=pl.ANY)] * 2
        args += list(prev)
    shape = (1, 2, rows, HD)
    each = pl.BlockSpec(shape, lambda h: (h, 0, 0, 0))
    specs, counts = [each] * 3, [heads] * 3
    if split > 0:
        specs.append(pl.BlockSpec(shape, lambda h: (jnp.minimum(h, split - 1), 0, 0, 0)))
        counts.append(split)
    if split < heads:
        specs.append(pl.BlockSpec(shape, lambda h: (jnp.maximum(h - split, 0), 0, 0, 0)))
        counts.append(heads - split)
    flops = 6 * 2 * rows * rows * BLOCKS * HD * GROUP * heads
    return pl.pallas_call(
        functools.partial(attend_kernel, split, heads),
        grid=(heads,),
        in_specs=in_specs,
        out_specs=[wide, wide] + specs,
        out_shape=[jax.ShapeDtypeStruct(q.shape, q.dtype)] * 2
        + [
            jax.ShapeDtypeStruct((n, 2, rows, HD), jnp.bfloat16 if i else jnp.float32)
            for i, n in enumerate(counts)
        ],
        scratch_shapes=[
            pltpu.VMEM((rows, BLOCKS * rows), jnp.float32),
            pltpu.VMEM((BLOCKS * rows, HD), jnp.bfloat16),
            pltpu.VMEM((BLOCKS * rows, HD), jnp.bfloat16),
            pltpu.VMEM((2, rows, BLOCKS * rows), jnp.float32),
            pltpu.VMEM((2, rows, BLOCKS * rows), jnp.bfloat16),
            pltpu.VMEM((2, rows, BLOCKS * rows), jnp.bfloat16),
        ],
        input_output_aliases=aliases,
        compiler_params=pltpu.CompilerParams(vmem_limit_bytes=48 * 1024 * 1024),
        cost_estimate=pl.CostEstimate(
            flops=flops, bytes_accessed=8 * 2**20, transcendentals=rows * rows * 4 * GROUP * heads
        ),
        name="attend",
    )(*args)


def finish_kernel(own, a, b, *refs):
    for part, ref in enumerate(refs[-2:]):
        for h in range(own.shape[0]):
            total = own[h, part] + a[h, part].astype(jnp.float32) + b[h, part].astype(jnp.float32)
            ref[:, h * HD : (h + 1) * HD] = total.astype(jnp.bfloat16)


def finish(first, heads, terms, prev):
    rows = terms[0][0].shape[2]
    unit = 2 if all(x % 2 == 0 for x in (first, heads, *[at for _, at in terms])) else 1
    specs = [
        pl.BlockSpec((unit, 2, rows, HD), lambda i, at=at: (at // unit + i, 0, 0, 0))
        for _, at in terms
    ]
    args, aliases = [t for t, _ in terms], {}
    out = pl.BlockSpec((rows, unit * HD), lambda i: (0, first // unit + i))
    if prev is not None:
        aliases = {3: 0, 4: 1}
        specs = specs + [pl.BlockSpec(memory_space=pl.ANY)] * 2
        args += list(prev)
    return pl.pallas_call(
        finish_kernel,
        grid=(heads // unit,),
        in_specs=specs,
        out_specs=[out, out],
        out_shape=[jax.ShapeDtypeStruct((rows, HK * HD), jnp.bfloat16)] * 2,
        input_output_aliases=aliases,
        cost_estimate=pl.CostEstimate(flops=10**6, bytes_accessed=3 * 2**20, transcendentals=0),
        name="finish",
    )(*args)


def shards(queries, keys, values, grad_out, segment_ids):
    rows = queries.shape[0]
    margin = REACH * rows
    first_row = lax.axis_index(AXES) * rows
    seg_pad = jnp.concatenate([jnp.full((margin,), -1, jnp.int32), segment_ids], 0)
    seg_row = lax.dynamic_slice_in_dim(seg_pad, first_row, margin + rows, 0)
    seg_col = seg_row[margin:].reshape(rows, 1)
    seg_row = seg_row.reshape(1, margin + rows)

    got = []
    for first, heads in GROUPS:
        cols = slice(first * HD, (first + heads) * HD)
        pack = jnp.stack([keys[:, cols], values[:, cols]])
        one = moved(pack, 1)
        three = moved(pack, 3)
        cut = heads // 2 * HD
        two = moved(one[:, :, :cut], 1), moved(three[:, :, cut:], -1)
        got.append((one, two, three))

    prev = None
    done = None
    tails = []
    for group, at, heads in CALLS:
        first, size = GROUPS[group]
        one, two, three = got[group]
        half = size // 2
        split = min(max(half - at, 0), heads)
        if 0 < split < heads:
            mid = (jnp.concatenate(two, 2), 0)
        else:
            mid = (two[0], at) if split else (two[1], at - half)
        asked = queries
        if prev is None:
            asked = after(queries, got[1][::2])
        if len(tails) == 3:
            asked = after(queries, [t[4] for t in tails[:2]])
        outs = attend(
            first + at, heads, split, seg_col, seg_row, asked, grad_out, keys, values,
            ((one, at), mid, (three, at)), prev,
        )
        prev, (own, keep, back1, *sent) = outs[:2], outs[2:]
        near = moved(back1, -1)
        if split:
            far = moved(sent[0], -3)
            relay = after((keep[:split] + near[:split]), far)
            tails.append((first + at, split, (own, 0), (far, 0), relay, -1))
        if split < heads:
            ahead = moved(sent[-1], 1)
            relay = after((keep[split:] + ahead), near)
            tails.append((first + at + split, heads - split, (own, split), (near, split), relay, -3))
    for first, heads, own, other, relay, steps in tails:
        done = finish(first, heads, (own, other, (moved(relay, steps), 0)), done)
    return prev[0], prev[1], done[0], done[1]


def solution(mesh):
    spec = P(AXES, None)
    return jax.shard_map(
        shards,
        mesh=mesh,
        in_specs=(spec, spec, spec, spec, P()),
        out_specs=(spec, spec, spec, spec),
        check_vma=False,
    )
```

```python
import functools

import jax
import jax.numpy as jnp
from jax import lax
from jax.experimental import pallas as pl
from jax.experimental.pallas import tpu as pltpu
from jax.sharding import PartitionSpec as P

HQ = 32
HK = 8
HD = 128
GROUP = HQ // HK
REACH = 3
BLOCKS = REACH + 1
AXES = ("dp", "cp")
LOG2E = 1.4426950408889634
HIDDEN = -1e30

GROUPS = ((0, 4), (4, 4))
CALLS = ((0, 0, 2), (0, 2, 2), (1, 0, 2), (1, 2, 2))


def moved(value, steps):
    count = lax.axis_size(AXES)
    return lax.ppermute(value, AXES, [(i, (i + steps) % count) for i in range(count)])


def after(value, gate):
    return lax.optimization_barrier((value, gate))[0]


def dot_nt(a, b):
    return lax.dot_general(a, b, (((1,), (1,)), ((), ())), preferred_element_type=jnp.float32)


def dot_nn(a, b):
    return jnp.dot(a, b, preferred_element_type=jnp.float32)


def attend_kernel(split, total, seg_col, seg_row, q, do, *refs):
    *outs, bias, kcat, vcat, scores, ph, ds = refs[2 * BLOCKS :]
    outs = outs[-(5 + (split > 0) + (split < total)) :]
    att, dq, own, keep, back1, *sent = outs
    rows = q.shape[0]
    scale = HD**-0.5

    @pl.when(pl.program_id(0) == 0)
    def _():
        for b in range(BLOCKS):
            at = (REACH - b) * rows
            seen = seg_col[...] == seg_row[:, at : at + rows]
            if b == 0:
                key_pos = lax.broadcasted_iota(jnp.int32, seen.shape, 1)
                seen &= key_pos <= lax.broadcasted_iota(jnp.int32, seen.shape, 0)
            bias[:, b * rows : (b + 1) * rows] = jnp.where(seen, 0.0, HIDDEN)

    for b in range(BLOCKS):
        kcat[b * rows : (b + 1) * rows, :] = refs[2 * b][...]
        vcat[b * rows : (b + 1) * rows, :] = refs[2 * b + 1][...]

    def score(g):
        qg = q[:, g * HD : (g + 1) * HD]
        scores[g % 2] = dot_nt(qg, kcat[...]) * (scale * LOG2E) + bias[...]

    def exponent(g):
        t = scores[g % 2]
        e = jnp.exp2(t - jnp.max(t, axis=1, keepdims=True))
        ph[g % 2] = e.astype(jnp.bfloat16)
        return 1.0 / jnp.sum(e, axis=1, keepdims=True)

    dk = dv = None
    score(0)
    inv = exponent(0)
    for g in range(GROUP):
        cols = slice(g * HD, (g + 1) * HD)
        if g + 1 < GROUP:
            score(g + 1)
        out = (dot_nn(ph[g % 2], vcat[...]) * inv).astype(jnp.bfloat16)
        att[:, cols] = out
        dog = (do[:, cols].astype(jnp.float32) * inv).astype(jnp.bfloat16)
        delta = jnp.sum(dog.astype(jnp.float32) * out.astype(jnp.float32), axis=1, keepdims=True)
        dp = dot_nt(dog, vcat[...])
        ds[g % 2] = ph[g % 2] * (dp - delta).astype(jnp.bfloat16)
        if g + 1 < GROUP:
            inv = exponent(g + 1)
        dq[:, cols] = (dot_nn(ds[g % 2], kcat[...]) * scale).astype(jnp.bfloat16)
        a, c = dot_nn(q[:, cols].T, ds[g % 2]), dot_nn(dog.T, ph[g % 2])
        dk = a if g == 0 else dk + a
        dv = c if g == 0 else dv + c

    def put(ref, b):
        at = slice(b * rows, (b + 1) * rows)
        ref[0, 0] = (dk[:, at] * scale).T.astype(ref.dtype)
        ref[0, 1] = dv[:, at].T.astype(ref.dtype)

    put(own, 0)

    def put_low():
        put(back1, 2)
        put(sent[0], 3)
        put(keep, 1)

    def put_high():
        put(back1, 1)
        put(sent[-1], 2)
        put(keep, 3)

    if split == total:
        put_low()
    elif split == 0:
        put_high()
    else:
        pl.when(pl.program_id(0) < split)(put_low)
        pl.when(pl.program_id(0) >= split)(put_high)


def attend(first, heads, split, seg_col, seg_row, q, do, k, v, received, prev):
    rows = q.shape[0]
    whole = lambda a: pl.BlockSpec(a.shape, lambda h: (0,) * a.ndim)
    wide = pl.BlockSpec((rows, GROUP * HD), lambda h: (0, first + h))
    own = pl.BlockSpec((rows, HD), lambda h: (0, first + h))
    in_specs = [whole(seg_col), whole(seg_row), wide, wide, own, own]
    args = [seg_col, seg_row, q, do, k, v]
    for block, at in received:
        for part in range(2):
            in_specs.append(
                pl.BlockSpec((None, rows, HD), lambda h, at=at, part=part: (part, 0, at + h))
            )
            args.append(block)
    aliases = {}
    if prev is not None:
        aliases = {len(args): 0, len(args) + 1: 1}
        in_specs += [pl.BlockSpec(memory_space=pl.ANY)] * 2
        args += list(prev)
    shape = (1, 2, rows, HD)
    each = pl.BlockSpec(shape, lambda h: (h, 0, 0, 0))
    specs, counts = [each] * 3, [heads] * 3
    if split > 0:
        specs.append(pl.BlockSpec(shape, lambda h: (jnp.minimum(h, split - 1), 0, 0, 0)))
        counts.append(split)
    if split < heads:
        specs.append(pl.BlockSpec(shape, lambda h: (jnp.maximum(h - split, 0), 0, 0, 0)))
        counts.append(heads - split)
    flops = 6 * 2 * rows * rows * BLOCKS * HD * GROUP * heads
    return pl.pallas_call(
        functools.partial(attend_kernel, split, heads),
        grid=(heads,),
        in_specs=in_specs,
        out_specs=[wide, wide] + specs,
        out_shape=[jax.ShapeDtypeStruct(q.shape, q.dtype)] * 2
        + [
            jax.ShapeDtypeStruct((n, 2, rows, HD), jnp.bfloat16 if i else jnp.float32)
            for i, n in enumerate(counts)
        ],
        scratch_shapes=[
            pltpu.VMEM((rows, BLOCKS * rows), jnp.float32),
            pltpu.VMEM((BLOCKS * rows, HD), jnp.bfloat16),
            pltpu.VMEM((BLOCKS * rows, HD), jnp.bfloat16),
            pltpu.VMEM((2, rows, BLOCKS * rows), jnp.float32),
            pltpu.VMEM((2, rows, BLOCKS * rows), jnp.bfloat16),
            pltpu.VMEM((2, rows, BLOCKS * rows), jnp.bfloat16),
        ],
        input_output_aliases=aliases,
        compiler_params=pltpu.CompilerParams(vmem_limit_bytes=60 * 1024 * 1024),
        cost_estimate=pl.CostEstimate(
            flops=flops, bytes_accessed=8 * 2**20, transcendentals=rows * rows * 4 * GROUP * heads
        ),
        name="attend",
    )(*args)


def shards(queries, keys, values, grad_out, segment_ids):
    rows = queries.shape[0]
    margin = REACH * rows
    first_row = lax.axis_index(AXES) * rows
    seg_pad = jnp.concatenate([jnp.full((margin,), -1, jnp.int32), segment_ids], 0)
    seg_row = lax.dynamic_slice_in_dim(seg_pad, first_row, margin + rows, 0)
    seg_col = seg_row[margin:].reshape(rows, 1)
    seg_row = seg_row.reshape(1, margin + rows)

    got = []
    for first, heads in GROUPS:
        cols = slice(first * HD, (first + heads) * HD)
        pack = jnp.stack([keys[:, cols], values[:, cols]])
        one = moved(pack, 1)
        three = moved(pack, 3)
        cut = heads // 2 * HD
        two = moved(one[:, :, :cut], 1), moved(three[:, :, cut:], -1)
        got.append((one, two, three))

    prev = None
    done = None
    tails = []
    for group, at, heads in CALLS:
        first, size = GROUPS[group]
        one, two, three = got[group]
        half = size // 2
        split = min(max(half - at, 0), heads)
        if 0 < split < heads:
            mid = (jnp.concatenate(two, 2), 0)
        else:
            mid = (two[0], at) if split else (two[1], at - half)
        asked = queries
        if prev is None:
            asked = after(queries, got[1][::2])
        if len(tails) == 3:
            asked = after(queries, [t[4] for t in tails[:2]])
        outs = attend(
            first + at, heads, split, seg_col, seg_row, asked, grad_out, keys, values,
            ((one, at), mid, (three, at)), prev,
        )
        prev, (own, keep, back1, *sent) = outs[:2], outs[2:]
        near = moved(back1, -1)
        if split:
            far = moved(sent[0], -3)
            relay = after((keep[:split] + near[:split]), far)
            tails.append((first + at, split, (own, 0), (far, 0), relay, -1))
        if split < heads:
            ahead = moved(sent[-1], 1)
            relay = after((keep[split:] + ahead), near)
            tails.append((first + at + split, heads - split, (own, split), (near, split), relay, -3))
    back = []
    for *_, relay, steps in tails:
        back.append(moved(relay, steps))
    sums = [
        (own[0] + other[0].astype(jnp.float32) + last.astype(jnp.float32)).astype(jnp.bfloat16)
        for (_, _, own, other, _, _), last in zip(tails, back)
    ]
    grads = []
    for part in range(2):
        wide = [jnp.concatenate([x[h, part] for h in range(x.shape[0])], 1) for x in sums]
        early = jnp.concatenate([*wide[:-1], jnp.zeros_like(wide[-1])], 1)
        early = lax.optimization_barrier(early)
        start = early.shape[1] - wide[-1].shape[1]
        grads.append(lax.dynamic_update_slice(early, wide[-1], (0, start)))
    return prev[0], prev[1], grads[0], grads[1]


def solution(mesh):
    spec = P(AXES, None)
    return jax.shard_map(
        shards,
        mesh=mesh,
        in_specs=(spec, spec, spec, spec, P()),
        out_specs=(spec, spec, spec, spec),
        check_vma=False,
    )
```
